32 devices in a mesh: section: 4 (over y, core), dp: 4 (over z), expert: 2 (over x).
Axes of the slice: x: 2, y: 2, z: 4, core: 2. Of those that a mesh axis runs over, the one named last changes fastest.
Arguments:
- stream: bfloat16 [4, 1024, 2048], P('section', ('dp', 'expert')), may hold values from -60 to 60
- norm_gain: bfloat16 [4, 2048], P('section'), may hold values from 0.29882812 to 3
- gate_probs: float32 [4, 1024, 8], P('section', ('dp', 'expert')), may hold values from 0.02 to 1
- expert_ids: int32 [4, 1024, 8], P('section', ('dp', 'expert')), may hold values from 0 to 127, as said below
- gate_up_weight: bfloat16 [4, 2, 2, 2048, 1024], P('section', 'expert', None, None, 'dp'), may hold values from -0.125 to 0.125
- down_weight: bfloat16 [4, 2, 1024, 2048], P('section', 'expert', 'dp'), may hold values from -0.1875 to 0.1875
Outputs:
- handed: bfloat16 [4, 1024, 2048], P('section', ('dp', 'expert'))
The draws below stay inside these ranges and needn't reach their ends.
Inputs may be any that keep to these rules, and one draw needn't show every extreme that they name: `expert_ids`: each row names 8 different experts. In the rows of one device each expert below 2 is named by at most 12 rows; in each section one such expert is named by exactly 12 rows in the rows of every device.
All inputs are finite; a program needn't handle non-finite values.
Results may differ from the reference program's by a relative error of at most 0.0077.
Values may be sent and summed in bfloat16 or wider, within the bound.
No kernel may reach another device: no remote copies, remote signals or barrier semaphores. Data moves between devices by JAX's collectives and lax.ppermute only.
A program may use at most 128 MiB of HBM per device.

```python
import math
import jax
import jax.numpy as jnp
from jax import lax

D = 2048
FFW = 1024
EXPERTS_ALL = 128
TOPK = 8
TOK_DEV = 128
HELD = 2
CAP = 12
TOKENS = 1024
N_SECTION = 4
N_DP = 4


def draw_stream(key, part):
    row_key, column_key, base_key = jax.random.split(key, 3)
    row_scales = jnp.exp(jax.random.uniform(row_key, (N_SECTION, TOKENS, 1), jnp.float32, jnp.log(0.3), jnp.log(3.0)))
    column_scales = jnp.exp(jax.random.uniform(column_key, (N_SECTION, 1, D), jnp.float32, jnp.log(0.5), jnp.log(5.0)))
    base_draw = jnp.clip(jax.random.normal(base_key, (N_SECTION, TOKENS, D), jnp.float32), -4.0, 4.0)
    widened = base_draw * row_scales * column_scales
    return widened.astype(jnp.bfloat16)


def draw_expert_ids(key, part):
    per_section = TOKENS // TOK_DEV
    block_count = N_SECTION * per_section
    others = EXPERTS_ALL - HELD
    slot_total = TOK_DEV * TOPK
    hot_key, low_key, spread_key, order_key, row_key = jax.random.split(key, 5)
    hottest = jax.random.randint(hot_key, (N_SECTION,), 0, HELD)
    hot_block = jnp.repeat(hottest, per_section)
    held_load = jax.random.randint(low_key, (block_count, HELD), 0, CAP + 1)
    held_load = jnp.where(jnp.arange(HELD)[None, :] == hot_block[:, None], CAP, held_load)
    remaining = slot_total - jnp.sum(held_load, axis=1)
    spread_keys = jax.random.split(spread_key, block_count)
    ranking = jax.vmap(lambda subkey: jax.random.permutation(subkey, others))(spread_keys)
    other_load = (remaining // others)[:, None] + (ranking < (remaining % others)[:, None]).astype(jnp.int32)
    loads = jnp.concatenate([held_load, other_load], axis=1)
    order_keys = jax.random.split(order_key, block_count)
    listing = jax.vmap(lambda subkey: jax.random.permutation(subkey, EXPERTS_ALL))(order_keys)
    listed_loads = jnp.take_along_axis(loads, listing, axis=1)
    bounds = jnp.cumsum(listed_loads, axis=1)
    spots = jnp.arange(slot_total, dtype=jnp.int32)
    located = jax.vmap(lambda bound_row: jnp.searchsorted(bound_row, spots, side='right'))(bounds)
    named = jnp.take_along_axis(listing, located, axis=1)
    row_keys = jax.random.split(row_key, block_count)
    row_order = jax.vmap(lambda subkey: jax.random.permutation(subkey, TOK_DEV))(row_keys)
    picks = row_order[:, :, None] + TOK_DEV * jnp.arange(TOPK, dtype=jnp.int32)[None, None, :]
    chosen = jnp.take_along_axis(named, picks.reshape(block_count, TOK_DEV * TOPK), axis=1)
    return chosen.reshape(N_SECTION, TOKENS, TOPK).astype(jnp.int32)


def levels(stream_key, dims, cuts, smallest, top_value):
    def one(dim, blocks):
        steps = jax.random.uniform(jax.random.fold_in(jax.random.fold_in(stream_key, 6), dim), (blocks,), jnp.float32, smallest / len(cuts), top_value / len(cuts))
        return jnp.repeat(jnp.exp(steps), dims[dim] // blocks).reshape((-1,) + (1,) * (len(dims) - dim - 1))

    gain = one(*cuts[0])
    for cut in cuts[1:]:
        gain = gain * one(*cut)
    return gain


def scatter_about(key, dims, spread, reach, pieces=(), kind=jnp.bfloat16):
    gain = levels(key, dims, pieces, -0.22, 0.18) if pieces else 1.0
    entries = jax.random.normal(key, dims, jnp.float32) * spread * gain
    return jnp.minimum(jnp.maximum(entries, -reach), reach).astype(kind)


def setup_inputs(seed: int = 0) -> dict:
    splits = jax.random.split(jax.random.key(seed), 7)
    return {
        "stream": draw_stream(jax.random.fold_in(splits[6], 71), 0),
        "norm_gain": jnp.clip(jnp.exp(math.log(3.0) - 2.306499 * jax.random.uniform(splits[1], (N_SECTION, D), jnp.float32) ** levels(splits[1], (N_SECTION, D), ((0, 4),), -0.2, 0.2)), 0.29882812, 3.0).astype(jnp.bfloat16),
        "gate_probs": jnp.clip(jnp.exp(math.log(1.0) - 3.912023 * jax.random.uniform(splits[2], (N_SECTION, TOKENS, TOPK), jnp.float32) ** levels(splits[2], (N_SECTION, TOKENS, TOPK), ((0, 4), (1, 8)), -0.2, 0.2)), 0.02, 1.0),
        "expert_ids": draw_expert_ids(jax.random.fold_in(splits[6], 71), 0),
        "gate_up_weight": scatter_about(splits[4], (N_SECTION, HELD, 2, D, FFW), D ** -0.5, 0.125, ((0, 4), (1, 2), (4, 4))),
        "down_weight": scatter_about(splits[5], (N_SECTION, HELD, FFW, D), FFW ** -0.5, 0.1875, ((0, 4), (1, 2), (2, 4))),
    }


epsilon = 1e-06

def normalize(activations, gain_row):
    widened = activations.astype(jnp.float32)
    inverse_rms = lax.rsqrt(lax.optimization_barrier(jnp.mean(widened * widened, axis=-1, keepdims=True)) + epsilon)
    return (widened * inverse_rms * gain_row.astype(jnp.float32)).astype(jnp.bfloat16)

def slot_tables(gate_probs, expert_ids, held_count, capacity):
    weights = gate_probs / lax.optimization_barrier(jnp.sum(gate_probs, axis=-1, keepdims=True))
    experts = jnp.arange(held_count, dtype=jnp.int32)
    matches = expert_ids[..., None] == experts
    coefficient = lax.optimization_barrier(jnp.sum(jnp.where(matches, weights[..., None], jnp.float32(0.0)), axis=-2))
    chosen = jnp.any(matches, axis=-2).astype(jnp.int32)
    position = jnp.cumsum(chosen, axis=-2) - chosen
    places = jnp.arange(capacity, dtype=jnp.int32)
    slot_table = (chosen[..., None] == 1) & (position[..., None] == places)
    return (coefficient, slot_table)

def expert_quarter(slot_rows, gate_matrix, up_matrix, down_matrix):
    gate_rows = jnp.dot(slot_rows, gate_matrix, preferred_element_type=jnp.float32)
    up_rows = jnp.dot(slot_rows, up_matrix, preferred_element_type=jnp.float32)
    hidden = (jax.nn.silu(gate_rows) * up_rows).astype(jnp.bfloat16)
    return jnp.dot(hidden, down_matrix, preferred_element_type=jnp.float32).astype(jnp.bfloat16)

def reference(stream, norm_gain, gate_probs, expert_ids, gate_up_weight, down_weight):
    block_count = TOKENS // TOK_DEV
    quarter = FFW // N_DP
    results = []
    for section_index in range(N_SECTION):
        normed = normalize(stream[section_index], norm_gain[section_index]).reshape(block_count, TOK_DEV, D)
        coefficient, slot_table = slot_tables(gate_probs[section_index].reshape(block_count, TOK_DEV, TOPK), expert_ids[section_index].reshape(block_count, TOK_DEV, TOPK), HELD, CAP)
        slot_onehot = slot_table.astype(jnp.float32)
        normed_wide = normed.astype(jnp.float32)
        section_gate_up = gate_up_weight[section_index]
        section_down = down_weight[section_index]

        def add_expert(expert, mixture):
            picked = lax.dynamic_index_in_dim(slot_onehot, expert, 2, keepdims=False)
            slot_rows = jnp.einsum('btc,btd->bcd', picked, normed_wide, precision=lax.Precision.HIGHEST).astype(jnp.bfloat16)
            slot_rows = slot_rows.reshape(block_count * CAP, D)
            weights_in = lax.dynamic_index_in_dim(section_gate_up, expert, 0, keepdims=False)
            weights_out = lax.dynamic_index_in_dim(section_down, expert, 0, keepdims=False)
            summed = jnp.zeros((block_count * CAP, D), jnp.float32)
            for part_index in range(N_DP):
                first = part_index * quarter
                partial_rows = expert_quarter(slot_rows, weights_in[0, :, first:first + quarter], weights_in[1, :, first:first + quarter], weights_out[first:first + quarter, :])
                summed = summed + partial_rows.astype(jnp.float32)
            rounded = lax.optimization_barrier(summed.astype(jnp.bfloat16)).astype(jnp.float32)
            shares = picked * lax.dynamic_index_in_dim(coefficient, expert, 2, keepdims=False)[..., None]
            return mixture + jnp.einsum('btc,bcd->btd', shares, rounded.reshape(block_count, CAP, D), precision=lax.Precision.HIGHEST)
        mixture = lax.fori_loop(0, HELD, add_expert, jnp.zeros((block_count, TOK_DEV, D), jnp.float32))
        results.append(mixture.reshape(TOKENS, D).astype(jnp.bfloat16))
    branches = jnp.stack(results)
    return jnp.roll(branches, 1, axis=0)
```

```python
import functools

import jax
import jax.numpy as jnp
from jax import lax
from jax.experimental import pallas as pl
from jax.experimental.pallas import tpu as pltpu
from jax.sharding import PartitionSpec as P

CAP = 12
GROUP = 2 * CAP
epsilon = 1e-06
f32 = jnp.float32
bf16 = jnp.bfloat16
VMEM_LIMIT = 40 * 1024 * 1024


def row_tables(rows, lanes):
    row = lax.broadcasted_iota(jnp.int32, (rows, lanes), 0) % GROUP
    left = (row < 8) | ((row >= 16) & (row < 20))
    slot = jnp.where(row < 8, row, jnp.where(row < 20, row - 8, row - 12))
    return left, slot


def swap_halves(value):
    pieces = []
    for first in range(0, value.shape[0], GROUP):
        pieces.append(value[first + 8 : first + 16])
        pieces.append(value[first : first + 8])
        pieces.append(pltpu.roll(value[first + 16 : first + 24], 4, 0))
    return jnp.concatenate(pieces, axis=0)


def dot(left, right):
    return jnp.dot(left, right, preferred_element_type=f32)


def pack_kernel(base_ref, stream_ref, gain_ref, probs_ref, ids_ref, meta_ref, *packed_refs, held_count):
    ids = ids_ref[...]
    probs = probs_ref[...]
    weights = probs / jnp.sum(probs, axis=0, keepdims=True)
    tokens = ids.shape[1]
    half = stream_ref.shape[1] // 2
    chosen, coefficients = [], []
    for block in range(held_count):
        matches = ids == lax.rem(base_ref[0] + block, held_count)
        coefficients.append(jnp.sum(jnp.where(matches, weights, 0.0), axis=0, keepdims=True))
        chosen.append(jnp.sum(jnp.where(matches, 1.0, 0.0), axis=0, keepdims=True))
    padding = -held_count % 8
    stacked = jnp.concatenate(chosen + [jnp.zeros((padding, tokens), f32)] * (padding > 0), axis=0)
    earlier = lax.broadcasted_iota(jnp.int32, (tokens, tokens), 0) < lax.broadcasted_iota(
        jnp.int32, (tokens, tokens), 1
    )
    counted = dot(stacked.astype(bf16), jnp.where(earlier, 1.0, 0.0).astype(bf16))
    position = jnp.where(stacked > 0.5, counted, -1.0)
    rows = held_count * GROUP
    left, slot = row_tables(rows, tokens)
    spread = jnp.concatenate(
        [jnp.broadcast_to(position[e : e + 1], (GROUP, tokens)) for e in range(held_count)], axis=0
    )
    onehot = slot.astype(f32) == spread
    packed = dot(jnp.where(onehot & left, 1.0, 0.0).astype(bf16), stream_ref[:, :half])
    packed += dot(jnp.where(onehot & ~left, 1.0, 0.0).astype(bf16), stream_ref[:, half:])
    squares = packed * packed
    total = jnp.sum(squares + swap_halves(squares), axis=1, keepdims=True)
    inverse_rms = lax.rsqrt(total / (2 * half) + epsilon)
    gain = gain_ref[...].astype(f32)
    left, _ = row_tables(rows, half)
    normed = packed * inverse_rms * jnp.where(left, gain[:, :half], gain[:, half:])
    per_ref = rows // len(packed_refs)
    for index, ref in enumerate(packed_refs):
        ref[...] = normed[index * per_ref : (index + 1) * per_ref].astype(bf16)
    lines = []
    for block in range(held_count):
        rest = coefficients[block]
        for _ in range(3):
            piece = rest.astype(bf16).astype(f32)
            lines.append(piece)
            rest = rest - piece
        lines.append(position[block : block + 1])
    table = jnp.concatenate(lines, axis=0)
    meta_ref[...] = table.astype(bf16)


def pack(stream, gain, probs, ids, base, held_count, outputs):
    tokens, width = stream.shape
    rows = held_count * GROUP // outputs
    whole = pl.BlockSpec(memory_space=pltpu.VMEM)
    return pl.pallas_call(
        functools.partial(pack_kernel, held_count=held_count),
        out_shape=[jax.ShapeDtypeStruct((4 * held_count, tokens), bf16)]
        + [jax.ShapeDtypeStruct((rows, width // 2), bf16)] * outputs,
        in_specs=[pl.BlockSpec(memory_space=pltpu.SMEM)] + [whole] * 4,
        out_specs=[whole] * (1 + outputs),
        compiler_params=pltpu.CompilerParams(vmem_limit_bytes=VMEM_LIMIT),
        cost_estimate=pl.CostEstimate(flops=2 * rows * tokens * width, bytes_accessed=2 * tokens * width, transcendentals=0),
    )(base, stream, gain, probs, ids)


def expert_rows(value, gate_ref, up_ref, down_ref):
    half = value.shape[1]
    value = value.astype(f32)
    swapped = swap_halves(value)
    left, _ = row_tables(*value.shape)
    first = jnp.where(left, value, swapped).astype(bf16)
    second = jnp.where(left, swapped, value).astype(bf16)
    gate = dot(first, gate_ref[:half]) + dot(second, gate_ref[half:])
    up = dot(first, up_ref[:half]) + dot(second, up_ref[half:])
    hidden = (gate / (1.0 + jnp.exp(-gate)) * up).astype(bf16)
    result = dot(hidden, down_ref[...])
    return jnp.where(left, result[:, :half], result[:, half:])


def expert_kernel(gate_up_ref, down_ref, *refs, count):
    value = jnp.concatenate([ref[...].astype(f32) for ref in refs[:count]], axis=0)
    result = expert_rows(value, gate_up_ref.at[0], gate_up_ref.at[1], down_ref)
    first = 0
    for ref in refs[count:]:
        ref[...] = result[first : first + ref.shape[0]].astype(bf16)
        first += ref.shape[0]


def expert_quarter(blocks, out_rows, gate_up, down):
    width = blocks[0].shape[1]
    rows = sum(block.shape[0] for block in blocks)
    whole = pl.BlockSpec(memory_space=pltpu.VMEM)
    return pl.pallas_call(
        functools.partial(expert_kernel, count=len(blocks)),
        out_shape=[jax.ShapeDtypeStruct((count, width), bf16) for count in out_rows],
        in_specs=[whole] * (2 + len(blocks)),
        out_specs=[whole] * len(out_rows),
        compiler_params=pltpu.CompilerParams(vmem_limit_bytes=VMEM_LIMIT),
        cost_estimate=pl.CostEstimate(
            flops=rows * 3 * down.size, bytes_accessed=2 * (gate_up.size + down.size), transcendentals=rows * down.shape[0]
        ),
    )(gate_up, down, *blocks)


def many_kernel(gate_up_ref, down_ref, in_ref, out_ref):
    out_ref[...] = expert_rows(in_ref[...], gate_up_ref.at[0], gate_up_ref.at[1], down_ref).astype(bf16)


def expert_quarter_many(block, gate_up, down):
    rows, width = block.shape
    step = GROUP * 4 if rows % (GROUP * 4) == 0 else rows
    return pl.pallas_call(
        many_kernel,
        grid=(rows // step,),
        out_shape=jax.ShapeDtypeStruct((rows, width), bf16),
        in_specs=[
            pl.BlockSpec(gate_up.shape, lambda i: (0, 0, 0)),
            pl.BlockSpec(down.shape, lambda i: (0, 0)),
            pl.BlockSpec((step, width), lambda i: (i, 0)),
        ],
        out_specs=pl.BlockSpec((step, width), lambda i: (i, 0)),
        compiler_params=pltpu.CompilerParams(vmem_limit_bytes=VMEM_LIMIT),
    )(gate_up, down, block)


def mix_kernel(meta_ref, *refs, held_count):
    rows_refs, out_ref = refs[:-1], refs[-1]
    half = out_ref.shape[1] // 2
    tokens = out_ref.shape[0]
    meta = meta_ref[:, :tokens].astype(f32)
    left, slot = row_tables(GROUP, tokens)
    blocks = []
    for ref in rows_refs:
        value = ref[...].astype(f32)
        for first in range(0, value.shape[0] // GROUP * GROUP, GROUP):
            blocks.append(value[first : first + GROUP])
    values = jnp.concatenate(blocks[:held_count], axis=0).astype(bf16)
    sides = [jnp.zeros((tokens, half), f32)] * 2
    for piece in range(3):
        tables = [[], []]
        for block in range(held_count):
            position = meta[4 * block + 3 : 4 * block + 4]
            share = meta[4 * block + piece : 4 * block + piece + 1]
            held = slot.astype(f32) == position
            tables[0].append(jnp.where(held & left, share, 0.0))
            tables[1].append(jnp.where(held & ~left, share, 0.0))
        for side in range(2):
            table = jnp.concatenate(tables[side], axis=0)
            sides[side] = sides[side] + dot(table.T.astype(bf16), values)
    out_ref[:, :half] = sides[0].astype(bf16)
    out_ref[:, half:] = sides[1].astype(bf16)


def mix(meta, blocks, tokens, held_count):
    width = blocks[0].shape[1]
    whole = pl.BlockSpec(memory_space=pltpu.VMEM)
    return pl.pallas_call(
        functools.partial(mix_kernel, held_count=held_count),
        out_shape=jax.ShapeDtypeStruct((tokens, 2 * width), bf16),
        in_specs=[whole] * (1 + len(blocks)),
        out_specs=whole,
        compiler_params=pltpu.CompilerParams(vmem_limit_bytes=VMEM_LIMIT),
    )(meta, *blocks)


def move(value, axes, target):
    sizes = [lax.axis_size(axis) for axis in axes]
    pairs = []
    total = 1
    for size in sizes:
        total *= size
    for source in range(total):
        rest, place = source, []
        for size in reversed(sizes):
            place.insert(0, rest % size)
            rest //= size
        index = 0
        for size, coordinate in zip(sizes, target(*place)):
            index = index * size + coordinate % size
        pairs.append((source, index))
    return lax.ppermute(value, axes if len(axes) > 1 else axes[0], pairs)


def across(value, step):
    return move(value, ("dp",), lambda q: (q ^ step,))


def added(values):
    total = values[0].astype(f32)
    for value in values[1:]:
        total = total + value.astype(f32)
    return total.astype(bf16)


def pair_shards(stream, gain, probs, ids, gate_up, down):
    base = lax.axis_index("expert").astype(jnp.int32).reshape(1)
    meta, own, other = pack(stream, gain, probs, ids, base, 2, 2)
    other = move(other, ("expert",), lambda e: (e ^ 1,))
    own3, own2 = across(own, 3), across(own, 2)
    other3, other2 = across(other, 3), across(other, 2)
    both1 = across(jnp.concatenate([own, other], axis=0), 1)
    part0, part3 = expert_quarter([own, other, own3, other3], [2 * GROUP] * 2, gate_up, down)
    back3 = across(part3, 3)
    part2, part1 = expert_quarter([own2, other2, both1], [2 * GROUP] * 2, gate_up, down)
    back2, back1 = across(part2, 2), across(part1, 1)
    summed = added([part0, back1, back2, back3])
    tagged = jnp.concatenate(
        [summed[:GROUP], jnp.pad(meta, ((0, 0), (0, summed.shape[1] - meta.shape[1])))], axis=0
    )
    tagged = move(tagged, ("section",), lambda s: (s + 1,))
    crossed = move(summed[GROUP:], ("section", "expert"), lambda s, e: (s + 1, e ^ 1))
    return mix(tagged[GROUP:], [tagged[:GROUP], crossed], stream.shape[0], 2)


def many_shards(stream, gain, probs, ids, gate_up, down):
    held_count = lax.axis_size("expert")
    group_count = lax.axis_size("dp")
    base = jnp.zeros((1,), jnp.int32)
    meta, packed = pack(stream, gain, probs, ids, base, held_count, 1)
    meta = move(meta, ("section",), lambda s: (s + 1,))
    shape = packed.shape
    split = (held_count, GROUP, shape[1])

    def exchanged(value):
        return lax.all_to_all(value.reshape(split), "expert", split_axis=0, concat_axis=0, tiled=True).reshape(shape)

    def shifted(value, step):
        return move(value, ("dp",), lambda q: (q + step,))

    received = exchanged(packed)
    parts = [expert_quarter_many(received, gate_up, down)]
    for step in range(1, group_count):
        parts.append(shifted(expert_quarter_many(shifted(received, step), gate_up, down), -step))
    summed = move(exchanged(added(parts)), ("section",), lambda s: (s + 1,))
    return mix(meta, [summed], stream.shape[0], held_count)


def shards(stream, norm_gain, gate_probs, expert_ids, gate_up_weight, down_weight):
    paired = lax.axis_size("expert") == 2 and lax.axis_size("dp") == 4
    body = pair_shards if paired else many_shards
    return body(
        stream[0], norm_gain, gate_probs[0].T, expert_ids[0].T, gate_up_weight[0, 0], down_weight[0, 0]
    )[None]


def solution(mesh):
    in_specs = (
        P("section", ("dp", "expert"), None),
        P("section", None),
        P("section", ("dp", "expert"), None),
        P("section", ("dp", "expert"), None),
        P("section", "expert", None, None, "dp"),
        P("section", "expert", "dp", None),
    )
    out_specs = P("section", ("dp", "expert"), None)
    return jax.shard_map(shards, mesh=mesh, in_specs=in_specs, out_specs=out_specs, check_vma=False)
```

```python
import functools

import jax
import jax.numpy as jnp
from jax import lax
from jax.experimental import pallas as pl
from jax.experimental.pallas import tpu as pltpu
from jax.sharding import PartitionSpec as P

CAP = 12
GROUP = 2 * CAP
epsilon = 1e-06
f32 = jnp.float32
bf16 = jnp.bfloat16
VMEM_LIMIT = 40 * 1024 * 1024


def row_tables(rows, lanes):
    row = lax.broadcasted_iota(jnp.int32, (rows, lanes), 0) % GROUP
    left = (row < 8) | ((row >= 16) & (row < 20))
    slot = jnp.where(row < 8, row, jnp.where(row < 20, row - 8, row - 12))
    return left, slot


def swap_halves(value):
    pieces = []
    for first in range(0, value.shape[0], GROUP):
        pieces.append(value[first + 8 : first + 16])
        pieces.append(value[first : first + 8])
        pieces.append(pltpu.roll(value[first + 16 : first + 24], 4, 0))
    return jnp.concatenate(pieces, axis=0)


def dot(left, right):
    return jnp.dot(left, right, preferred_element_type=f32)


def pack_kernel(base_ref, stream_hbm, gain_hbm, probs_hbm, ids_hbm, meta_ref, *refs, held_count):
    packed_refs = refs[:-5]
    stream_ref, gain_ref, probs_ref, ids_ref, sems = refs[-5:]
    copies = [
        pltpu.make_async_copy(source, target, sems.at[index])
        for index, (source, target) in enumerate(
            ((ids_hbm, ids_ref), (probs_hbm, probs_ref), (stream_hbm, stream_ref), (gain_hbm, gain_ref))
        )
    ]
    for copy in copies:
        copy.start()
    copies[0].wait()
    copies[1].wait()
    ids = ids_ref[...]
    probs = probs_ref[...]
    weights = probs / jnp.sum(probs, axis=0, keepdims=True)
    tokens = ids.shape[1]
    half = stream_ref.shape[1] // 2
    chosen, coefficients = [], []
    for block in range(held_count):
        matches = ids == lax.rem(base_ref[0] + block, held_count)
        coefficients.append(jnp.sum(jnp.where(matches, weights, 0.0), axis=0, keepdims=True))
        chosen.append(jnp.sum(jnp.where(matches, 1.0, 0.0), axis=0, keepdims=True))
    padding = -held_count % 8
    stacked = jnp.concatenate(chosen + [jnp.zeros((padding, tokens), f32)] * (padding > 0), axis=0)
    earlier = lax.broadcasted_iota(jnp.int32, (tokens, tokens), 0) < lax.broadcasted_iota(
        jnp.int32, (tokens, tokens), 1
    )
    counted = dot(stacked.astype(bf16), jnp.where(earlier, 1.0, 0.0).astype(bf16))
    position = jnp.where(stacked > 0.5, counted, -1.0)
    rows = held_count * GROUP
    left, slot = row_tables(rows, tokens)
    spread = jnp.concatenate(
        [jnp.broadcast_to(position[e : e + 1], (GROUP, tokens)) for e in range(held_count)], axis=0
    )
    onehot = slot.astype(f32) == spread
    lines = []
    for block in range(held_count):
        rest = coefficients[block]
        for _ in range(3):
            piece = rest.astype(bf16).astype(f32)
            lines.append(piece)
            rest = rest - piece
        lines.append(position[block : block + 1])
    meta_ref[...] = jnp.concatenate(lines, axis=0).astype(bf16)
    copies[2].wait()
    packed = dot(jnp.where(onehot & left, 1.0, 0.0).astype(bf16), stream_ref[:, :half])
    packed += dot(jnp.where(onehot & ~left, 1.0, 0.0).astype(bf16), stream_ref[:, half:])
    squares = packed * packed
    total = jnp.sum(squares + swap_halves(squares), axis=1, keepdims=True)
    inverse_rms = lax.rsqrt(total / (2 * half) + epsilon)
    copies[3].wait()
    gain = gain_ref[...].astype(f32)
    left, _ = row_tables(rows, half)
    normed = packed * inverse_rms * jnp.where(left, gain[:, :half], gain[:, half:])
    per_ref = rows // len(packed_refs)
    for index, ref in enumerate(packed_refs):
        ref[...] = normed[index * per_ref : (index + 1) * per_ref].astype(bf16)


def pack(stream, gain, probs, ids, base, held_count, outputs):
    tokens, width = stream.shape
    rows = held_count * GROUP // outputs
    whole = pl.BlockSpec(memory_space=pltpu.VMEM)
    far = pl.BlockSpec(memory_space=pltpu.HBM)
    return pl.pallas_call(
        functools.partial(pack_kernel, held_count=held_count),
        out_shape=[jax.ShapeDtypeStruct((4 * held_count, tokens), bf16)]
        + [jax.ShapeDtypeStruct((rows, width // 2), bf16)] * outputs,
        in_specs=[pl.BlockSpec(memory_space=pltpu.SMEM)] + [far] * 4,
        out_specs=[whole] * (1 + outputs),
        scratch_shapes=[pltpu.VMEM(array.shape, array.dtype) for array in (stream, gain, probs, ids)]
        + [pltpu.SemaphoreType.DMA((4,))],
        compiler_params=pltpu.CompilerParams(vmem_limit_bytes=VMEM_LIMIT),
        cost_estimate=pl.CostEstimate(flops=2 * rows * tokens * width, bytes_accessed=2 * tokens * width, transcendentals=0),
    )(base, *[pltpu.with_memory_space_constraint(array, pltpu.HBM) for array in (stream, gain, probs, ids)])


def load_kernel(gate_up_hbm, down_hbm, after_ref, gate_up_ref, down_ref, sems):
    copies = [
        pltpu.make_async_copy(gate_up_hbm, gate_up_ref, sems.at[0]),
        pltpu.make_async_copy(down_hbm, down_ref, sems.at[1]),
    ]
    for copy in copies:
        copy.start()
    for copy in copies:
        copy.wait()


def load(gate_up, down, after):
    whole = pl.BlockSpec(memory_space=pltpu.VMEM)
    far = pl.BlockSpec(memory_space=pltpu.HBM)
    return pl.pallas_call(
        load_kernel,
        out_shape=[jax.ShapeDtypeStruct(gate_up.shape, bf16), jax.ShapeDtypeStruct(down.shape, bf16)],
        in_specs=[far, far, pl.BlockSpec(memory_space=pl.ANY)],
        out_specs=[whole, whole],
        scratch_shapes=[pltpu.SemaphoreType.DMA((2,))],
        compiler_params=pltpu.CompilerParams(vmem_limit_bytes=VMEM_LIMIT),
        cost_estimate=pl.CostEstimate(flops=0, bytes_accessed=2 * (gate_up.size + down.size), transcendentals=0),
    )(*[pltpu.with_memory_space_constraint(array, pltpu.HBM) for array in (gate_up, down)], after)


def expert_rows(value, gate_ref, up_ref, down_ref):
    half = value.shape[1]
    value = value.astype(f32)
    swapped = swap_halves(value)
    left, _ = row_tables(*value.shape)
    first = jnp.where(left, value, swapped).astype(bf16)
    second = jnp.where(left, swapped, value).astype(bf16)
    gate = dot(first, gate_ref[:half]) + dot(second, gate_ref[half:])
    up = dot(first, up_ref[:half]) + dot(second, up_ref[half:])
    hidden = (gate / (1.0 + jnp.exp(-gate)) * up).astype(bf16)
    result = dot(hidden, down_ref[...])
    return jnp.where(left, result[:, :half], result[:, half:])


def expert_kernel(gate_up_ref, down_ref, *refs, count):
    value = jnp.concatenate([ref[...].astype(f32) for ref in refs[:count]], axis=0)
    result = expert_rows(value, gate_up_ref.at[0], gate_up_ref.at[1], down_ref)
    first = 0
    for ref in refs[count:]:
        ref[...] = result[first : first + ref.shape[0]].astype(bf16)
        first += ref.shape[0]


def expert_quarter(blocks, out_rows, gate_up, down):
    width = blocks[0].shape[1]
    rows = sum(block.shape[0] for block in blocks)
    whole = pl.BlockSpec(memory_space=pltpu.VMEM)
    return pl.pallas_call(
        functools.partial(expert_kernel, count=len(blocks)),
        out_shape=[jax.ShapeDtypeStruct((count, width), bf16) for count in out_rows],
        in_specs=[whole] * (2 + len(blocks)),
        out_specs=[whole] * len(out_rows),
        compiler_params=pltpu.CompilerParams(vmem_limit_bytes=VMEM_LIMIT),
        cost_estimate=pl.CostEstimate(
            flops=rows * 3 * down.size, bytes_accessed=2 * (gate_up.size + down.size), transcendentals=rows * down.shape[0]
        ),
    )(gate_up, down, *blocks)


def many_kernel(gate_up_ref, down_ref, in_ref, out_ref):
    out_ref[...] = expert_rows(in_ref[...], gate_up_ref.at[0], gate_up_ref.at[1], down_ref).astype(bf16)


def expert_quarter_many(block, gate_up, down):
    rows, width = block.shape
    step = GROUP * 4 if rows % (GROUP * 4) == 0 else rows
    return pl.pallas_call(
        many_kernel,
        grid=(rows // step,),
        out_shape=jax.ShapeDtypeStruct((rows, width), bf16),
        in_specs=[
            pl.BlockSpec(gate_up.shape, lambda i: (0, 0, 0)),
            pl.BlockSpec(down.shape, lambda i: (0, 0)),
            pl.BlockSpec((step, width), lambda i: (i, 0)),
        ],
        out_specs=pl.BlockSpec((step, width), lambda i: (i, 0)),
        compiler_params=pltpu.CompilerParams(vmem_limit_bytes=VMEM_LIMIT),
    )(gate_up, down, block)


def mix_kernel(meta_ref, *refs, held_count):
    rows_refs, out_hbm, out_ref, sems = refs[:-3], refs[-3], refs[-2], refs[-1]
    tokens, width = out_ref.shape
    half = width // 2
    meta = meta_ref[:, :tokens].astype(f32)
    _, slot = row_tables(GROUP, tokens)
    values = jnp.concatenate([ref[...].astype(f32) for ref in rows_refs], axis=0)
    left, _ = row_tables(*values.shape)
    sides = [jnp.where(left, values, 0.0).astype(bf16), jnp.where(left, 0.0, values).astype(bf16)]
    held = [slot.astype(f32) == meta[4 * block + 3 : 4 * block + 4] for block in range(held_count)]
    tables = []
    for piece in range(3):
        table = jnp.concatenate(
            [
                jnp.where(held[block], meta[4 * block + piece : 4 * block + piece + 1], 0.0)
                for block in range(held_count)
            ],
            axis=0,
        )
        tables.append(table.T.astype(bf16))
    copies = []
    for side in range(2):
        columns = pl.ds(side * half, half)
        total = sum(dot(table, sides[side]) for table in tables)
        out_ref[:, columns] = total.astype(bf16)
        copies.append(pltpu.make_async_copy(out_ref.at[:, columns], out_hbm.at[:, columns], sems.at[side]))
        copies[side].start()
    for copy in copies:
        copy.wait()


def mix(meta, blocks, tokens, held_count):
    width = blocks[0].shape[1]
    whole = pl.BlockSpec(memory_space=pltpu.VMEM)
    return pl.pallas_call(
        functools.partial(mix_kernel, held_count=held_count),
        out_shape=jax.ShapeDtypeStruct((tokens, 2 * width), bf16),
        in_specs=[whole] * (1 + len(blocks)),
        out_specs=pl.BlockSpec(memory_space=pltpu.HBM),
        scratch_shapes=[pltpu.VMEM((tokens, 2 * width), bf16), pltpu.SemaphoreType.DMA((2,))],
        compiler_params=pltpu.CompilerParams(vmem_limit_bytes=VMEM_LIMIT),
    )(meta, *blocks)


def move(value, axes, target):
    sizes = [lax.axis_size(axis) for axis in axes]
    pairs = []
    total = 1
    for size in sizes:
        total *= size
    for source in range(total):
        rest, place = source, []
        for size in reversed(sizes):
            place.insert(0, rest % size)
            rest //= size
        index = 0
        for size, coordinate in zip(sizes, target(*place)):
            index = index * size + coordinate % size
        pairs.append((source, index))
    return lax.ppermute(value, axes if len(axes) > 1 else axes[0], pairs)


def across(value, step):
    return move(value, ("dp",), lambda q: (q ^ step,))


def added(values):
    total = values[0].astype(f32)
    for value in values[1:]:
        total = total + value.astype(f32)
    return total.astype(bf16)


def pair_shards(stream, gain, probs, ids, gate_up, down):
    base = lax.axis_index("expert").astype(jnp.int32).reshape(1)
    meta, own, other = pack(stream, gain, probs, ids, base, 2, 2)
    gate_up, down = load(gate_up, down, own)
    other = move(other, ("expert",), lambda e: (e ^ 1,))
    own3, own2 = across(own, 3), across(own, 2)
    other3, other2 = across(other, 3), across(other, 2)
    both1 = across(jnp.concatenate([own, other], axis=0), 1)
    part0, part3 = expert_quarter([own, other, own3, other3], [2 * GROUP] * 2, gate_up, down)
    back3 = across(part3, 3)
    part2, part1 = expert_quarter([own2, other2, both1], [2 * GROUP] * 2, gate_up, down)
    back2, back1 = across(part2, 2), across(part1, 1)
    summed = added([part0, back1, back2, back3])
    tagged = jnp.concatenate(
        [summed[:GROUP], jnp.pad(meta, ((0, 0), (0, summed.shape[1] - meta.shape[1])))], axis=0
    )
    tagged = move(tagged, ("section",), lambda s: (s + 1,))
    crossed = move(summed[GROUP:], ("section", "expert"), lambda s, e: (s + 1, e ^ 1))
    return mix(tagged[GROUP:], [tagged[:GROUP], crossed], stream.shape[0], 2)


def many_shards(stream, gain, probs, ids, gate_up, down):
    held_count = lax.axis_size("expert")
    group_count = lax.axis_size("dp")
    base = jnp.zeros((1,), jnp.int32)
    meta, packed = pack(stream, gain, probs, ids, base, held_count, 1)
    meta = move(meta, ("section",), lambda s: (s + 1,))
    shape = packed.shape
    split = (held_count, GROUP, shape[1])

    def exchanged(value):
        return lax.all_to_all(value.reshape(split), "expert", split_axis=0, concat_axis=0, tiled=True).reshape(shape)

    def shifted(value, step):
        return move(value, ("dp",), lambda q: (q + step,))

    received = exchanged(packed)
    parts = [expert_quarter_many(received, gate_up, down)]
    for step in range(1, group_count):
        parts.append(shifted(expert_quarter_many(shifted(received, step), gate_up, down), -step))
    summed = move(exchanged(added(parts)), ("section",), lambda s: (s + 1,))
    return mix(meta, [summed], stream.shape[0], held_count)


def shards(stream, norm_gain, gate_probs, expert_ids, gate_up_weight, down_weight):
    paired = lax.axis_size("expert") == 2 and lax.axis_size("dp") == 4
    body = pair_shards if paired else many_shards
    return body(
        stream[0], norm_gain, gate_probs[0].T, expert_ids[0].T, gate_up_weight[0, 0], down_weight[0, 0]
    )[None]


def solution(mesh):
    in_specs = (
        P("section", ("dp", "expert"), None),
        P("section", None),
        P("section", ("dp", "expert"), None),
        P("section", ("dp", "expert"), None),
        P("section", "expert", None, None, "dp"),
        P("section", "expert", "dp", None),
    )
    out_specs = P("section", ("dp", "expert"), None)
    return jax.shard_map(shards, mesh=mesh, in_specs=in_specs, out_specs=out_specs, check_vma=False)
```

```python
import functools

import jax
import jax.numpy as jnp
from jax import lax
from jax.experimental import pallas as pl
from jax.experimental.pallas import tpu as pltpu
from jax.sharding import PartitionSpec as P

CAP = 12
GROUP = 2 * CAP
epsilon = 1e-06
f32 = jnp.float32
bf16 = jnp.bfloat16
LOAD_PIECES = 2
MIX_PIECES = 2
VMEM_LIMIT = 40 * 1024 * 1024


def row_tables(rows, lanes):
    row = lax.broadcasted_iota(jnp.int32, (rows, lanes), 0) % GROUP
    left = (row < 8) | ((row >= 16) & (row < 20))
    slot = jnp.where(row < 8, row, jnp.where(row < 20, row - 8, row - 12))
    return left, slot


def swap_halves(value):
    pieces = []
    for first in range(0, value.shape[0], GROUP):
        pieces.append(value[first + 8 : first + 16])
        pieces.append(value[first : first + 8])
        pieces.append(pltpu.roll(value[first + 16 : first + 24], 4, 0))
    return jnp.concatenate(pieces, axis=0)


def dot(left, right):
    return jnp.dot(left, right, preferred_element_type=f32)


def pack_kernel(base_ref, ids_hbm, probs_hbm, stream_hbm, gain_hbm, gate_up_hbm, down_hbm, meta_ref, *refs, held_count):
    packed_refs = refs[:-7]
    gate_up_ref, down_ref = refs[-7:-5]
    ids_ref, probs_ref, stream_ref, gain_ref, sems = refs[-5:]
    pairs = [(ids_hbm, ids_ref), (probs_hbm, probs_ref), (stream_hbm, stream_ref), (gain_hbm, gain_ref)]
    depth = gate_up_ref.shape[1] // LOAD_PIECES
    for matrix in range(2):
        for piece in range(LOAD_PIECES):
            place = (matrix, pl.ds(piece * depth, depth))
            pairs.append((gate_up_hbm.at[place], gate_up_ref.at[place]))
    depth = down_ref.shape[0] // LOAD_PIECES
    for piece in range(LOAD_PIECES):
        place = pl.ds(piece * depth, depth)
        pairs.append((down_hbm.at[place], down_ref.at[place]))
    copies = [
        pltpu.make_async_copy(source, target, sems.at[index]) for index, (source, target) in enumerate(pairs)
    ]
    for copy in copies:
        copy.start()
    copies[0].wait()
    copies[1].wait()
    ids = ids_ref[...]
    probs = probs_ref[...]
    weights = probs / jnp.sum(probs, axis=0, keepdims=True)
    tokens = ids.shape[1]
    half = stream_ref.shape[1] // 2
    chosen, coefficients = [], []
    for block in range(held_count):
        matches = ids == lax.rem(base_ref[0] + block, held_count)
        coefficients.append(jnp.sum(jnp.where(matches, weights, 0.0), axis=0, keepdims=True))
        chosen.append(jnp.sum(jnp.where(matches, 1.0, 0.0), axis=0, keepdims=True))
    padding = -held_count % 8
    stacked = jnp.concatenate(chosen + [jnp.zeros((padding, tokens), f32)] * (padding > 0), axis=0)
    earlier = lax.broadcasted_iota(jnp.int32, (tokens, tokens), 0) < lax.broadcasted_iota(
        jnp.int32, (tokens, tokens), 1
    )
    counted = dot(stacked.astype(bf16), jnp.where(earlier, 1.0, 0.0).astype(bf16))
    position = jnp.where(stacked > 0.5, counted, -1.0)
    rows = held_count * GROUP
    left, slot = row_tables(rows, tokens)
    spread = jnp.concatenate(
        [jnp.broadcast_to(position[e : e + 1], (GROUP, tokens)) for e in range(held_count)], axis=0
    )
    onehot = slot.astype(f32) == spread
    lines = []
    for block in range(held_count):
        rest = coefficients[block]
        for _ in range(3):
            piece = rest.astype(bf16).astype(f32)
            lines.append(piece)
            rest = rest - piece
        lines.append(position[block : block + 1])
    meta_ref[...] = jnp.concatenate(lines, axis=0).astype(bf16)
    copies[2].wait()
    packed = dot(jnp.where(onehot & left, 1.0, 0.0).astype(bf16), stream_ref[:, :half])
    packed += dot(jnp.where(onehot & ~left, 1.0, 0.0).astype(bf16), stream_ref[:, half:])
    squares = packed * packed
    total = jnp.sum(squares + swap_halves(squares), axis=1, keepdims=True)
    inverse_rms = lax.rsqrt(total / (2 * half) + epsilon)
    copies[3].wait()
    gain = gain_ref[...].astype(f32)
    left, _ = row_tables(rows, half)
    normed = packed * inverse_rms * jnp.where(left, gain[:, :half], gain[:, half:])
    per_ref = rows // len(packed_refs)
    for index, ref in enumerate(packed_refs):
        ref[...] = normed[index * per_ref : (index + 1) * per_ref].astype(bf16)
    for copy in copies[4:]:
        copy.wait()


def pack(stream, gain, probs, ids, gate_up, down, base, held_count, outputs):
    tokens, width = stream.shape
    rows = held_count * GROUP // outputs
    whole = pl.BlockSpec(memory_space=pltpu.VMEM)
    far = pl.BlockSpec(memory_space=pltpu.HBM)
    arrays = (ids, probs, stream, gain, gate_up, down)
    return pl.pallas_call(
        functools.partial(pack_kernel, held_count=held_count),
        out_shape=[jax.ShapeDtypeStruct((4 * held_count, tokens), bf16)]
        + [jax.ShapeDtypeStruct((rows, width // 2), bf16)] * outputs
        + [jax.ShapeDtypeStruct(gate_up.shape, bf16), jax.ShapeDtypeStruct(down.shape, bf16)],
        in_specs=[pl.BlockSpec(memory_space=pltpu.SMEM)] + [far] * len(arrays),
        out_specs=[whole] * (3 + outputs),
        scratch_shapes=[pltpu.VMEM(array.shape, array.dtype) for array in arrays[:4]]
        + [pltpu.SemaphoreType.DMA((4 + 3 * LOAD_PIECES,))],
        compiler_params=pltpu.CompilerParams(vmem_limit_bytes=VMEM_LIMIT),
    )(base, *[pltpu.with_memory_space_constraint(array, pltpu.HBM) for array in arrays])


def expert_rows(value, gate_ref, up_ref, down_ref):
    half = value.shape[1]
    value = value.astype(f32)
    swapped = swap_halves(value)
    left, _ = row_tables(*value.shape)
    first = jnp.where(left, value, swapped).astype(bf16)
    second = jnp.where(left, swapped, value).astype(bf16)
    gate = dot(first, gate_ref[:half]) + dot(second, gate_ref[half:])
    up = dot(first, up_ref[:half]) + dot(second, up_ref[half:])
    hidden = (gate / (1.0 + jnp.exp(-gate)) * up).astype(bf16)
    result = dot(hidden, down_ref[...])
    return jnp.where(left, result[:, :half], result[:, half:])


def expert_kernel(gate_up_ref, down_ref, *refs, count):
    value = jnp.concatenate([ref[...].astype(f32) for ref in refs[:count]], axis=0)
    result = expert_rows(value, gate_up_ref.at[0], gate_up_ref.at[1], down_ref)
    first = 0
    for ref in refs[count:]:
        ref[...] = result[first : first + ref.shape[0]].astype(bf16)
        first += ref.shape[0]


def expert_quarter(blocks, out_rows, gate_up, down):
    width = blocks[0].shape[1]
    whole = pl.BlockSpec(memory_space=pltpu.VMEM)
    return pl.pallas_call(
        functools.partial(expert_kernel, count=len(blocks)),
        out_shape=[jax.ShapeDtypeStruct((count, width), bf16) for count in out_rows],
        in_specs=[whole] * (2 + len(blocks)),
        out_specs=[whole] * len(out_rows),
        compiler_params=pltpu.CompilerParams(vmem_limit_bytes=VMEM_LIMIT),
    )(gate_up, down, *blocks)


def many_kernel(gate_up_ref, down_ref, in_ref, out_ref):
    out_ref[...] = expert_rows(in_ref[...], gate_up_ref.at[0], gate_up_ref.at[1], down_ref).astype(bf16)


def expert_quarter_many(block, gate_up, down):
    rows, width = block.shape
    step = GROUP * 4 if rows % (GROUP * 4) == 0 else rows
    return pl.pallas_call(
        many_kernel,
        grid=(rows // step,),
        out_shape=jax.ShapeDtypeStruct((rows, width), bf16),
        in_specs=[
            pl.BlockSpec(gate_up.shape, lambda i: (0, 0, 0)),
            pl.BlockSpec(down.shape, lambda i: (0, 0)),
            pl.BlockSpec((step, width), lambda i: (i, 0)),
        ],
        out_specs=pl.BlockSpec((step, width), lambda i: (i, 0)),
        compiler_params=pltpu.CompilerParams(vmem_limit_bytes=VMEM_LIMIT),
    )(gate_up, down, block)


def table_kernel(meta_ref, table_ref, *, held_count):
    tokens = table_ref.shape[0]
    meta = meta_ref[:, :tokens].astype(f32)
    _, slot = row_tables(GROUP, tokens)
    lines = []
    for piece in range(3):
        for block in range(held_count):
            position = meta[4 * block + 3 : 4 * block + 4]
            share = meta[4 * block + piece : 4 * block + piece + 1]
            lines.append(jnp.where(slot.astype(f32) == position, share, 0.0))
    table_ref[...] = jnp.concatenate(lines, axis=0).T.astype(bf16)


def share_table(meta, tokens, held_count):
    whole = pl.BlockSpec(memory_space=pltpu.VMEM)
    return pl.pallas_call(
        functools.partial(table_kernel, held_count=held_count),
        out_shape=jax.ShapeDtypeStruct((tokens, 3 * GROUP * held_count), bf16),
        in_specs=[whole],
        out_specs=whole,
        compiler_params=pltpu.CompilerParams(vmem_limit_bytes=VMEM_LIMIT),
    )(meta)


def mix_kernel(table_ref, *refs):
    rows_refs, out_hbm, out_ref, sems = refs[:-3], refs[-3], refs[-2], refs[-1]
    half = out_ref.shape[1] // 2
    values = jnp.concatenate([ref[...].astype(f32) for ref in rows_refs], axis=0)
    left, _ = row_tables(*values.shape)
    sides = [jnp.where(left, values, 0.0).astype(bf16), jnp.where(left, 0.0, values).astype(bf16)]
    copies = []
    for step in range(2 * MIX_PIECES):
        side, piece = divmod(step, MIX_PIECES)
        length = half // MIX_PIECES
        columns = pl.ds(step * length, length)
        value = sides[side][:, piece * length : (piece + 1) * length]
        total = dot(table_ref[...], jnp.concatenate([value] * 3, axis=0))
        out_ref[:, columns] = total.astype(bf16)
        copies.append(pltpu.make_async_copy(out_ref.at[:, columns], out_hbm.at[:, columns], sems.at[step]))
        copies[step].start()
    for copy in copies:
        copy.wait()


def mix(table, blocks):
    tokens = table.shape[0]
    width = blocks[0].shape[1]
    whole = pl.BlockSpec(memory_space=pltpu.VMEM)
    return pl.pallas_call(
        mix_kernel,
        out_shape=jax.ShapeDtypeStruct((tokens, 2 * width), bf16),
        in_specs=[whole] * (1 + len(blocks)),
        out_specs=pl.BlockSpec(memory_space=pltpu.HBM),
        scratch_shapes=[pltpu.VMEM((tokens, 2 * width), bf16), pltpu.SemaphoreType.DMA((2 * MIX_PIECES,))],
        compiler_params=pltpu.CompilerParams(vmem_limit_bytes=VMEM_LIMIT),
    )(table, *blocks)


def move(value, axes, target):
    sizes = [lax.axis_size(axis) for axis in axes]
    pairs = []
    total = 1
    for size in sizes:
        total *= size
    for source in range(total):
        rest, place = source, []
        for size in reversed(sizes):
            place.insert(0, rest % size)
            rest //= size
        index = 0
        for size, coordinate in zip(sizes, target(*place)):
            index = index * size + coordinate % size
        pairs.append((source, index))
    return lax.ppermute(value, axes if len(axes) > 1 else axes[0], pairs)


def across(value, step):
    return move(value, ("dp",), lambda q: (q ^ step,))


def added(values):
    total = values[0].astype(f32)
    for value in values[1:]:
        total = total + value.astype(f32)
    return total.astype(bf16)


def pair_shards(stream, gain, probs, ids, gate_up, down):
    base = lax.axis_index("expert").astype(jnp.int32).reshape(1)
    meta, own, other, gate_up, down = pack(stream, gain, probs, ids, gate_up, down, base, 2, 2)
    other = move(other, ("expert",), lambda e: (e ^ 1,))
    blocks = {0: [own, other]}
    for step in (3, 2, 1):
        blocks[step] = [across(own, step), across(other, step)]
    rows = 2 * GROUP
    part0, part1 = expert_quarter(blocks[0] + blocks[1], [rows, rows], gate_up, down)
    back2 = across(expert_quarter(blocks[2], [rows], gate_up, down)[0], 2)
    back3 = across(expert_quarter(blocks[3], [rows], gate_up, down)[0], 3)
    direct = move(part1[:GROUP], ("section", "dp"), lambda s, q: (s + 1, q ^ 1))
    direct_crossed = move(part1[GROUP:], ("section", "dp", "expert"), lambda s, q, e: (s + 1, q ^ 1, e ^ 1))
    summed = added([part0, back2, back3])
    wide = jnp.pad(meta, ((0, 0), (0, summed.shape[1] - meta.shape[1])))
    tagged = jnp.concatenate([summed[:GROUP], wide], axis=0)
    tagged = move(tagged, ("section",), lambda s: (s + 1,))
    crossed = move(summed[GROUP:], ("section", "expert"), lambda s, e: (s + 1, e ^ 1))
    table = share_table(tagged[GROUP:], stream.shape[0], 2)
    return mix(table, [added([tagged[:GROUP], direct]), added([crossed, direct_crossed])])


def many_shards(stream, gain, probs, ids, gate_up, down):
    held_count = lax.axis_size("expert")
    group_count = lax.axis_size("dp")
    base = jnp.zeros((1,), jnp.int32)
    meta, packed, gate_up, down = pack(stream, gain, probs, ids, gate_up, down, base, held_count, 1)
    meta = move(meta, ("section",), lambda s: (s + 1,))
    shape = packed.shape
    split = (held_count, GROUP, shape[1])

    def exchanged(value):
        return lax.all_to_all(value.reshape(split), "expert", split_axis=0, concat_axis=0, tiled=True).reshape(shape)

    def shifted(value, step):
        return move(value, ("dp",), lambda q: (q + step,))

    received = exchanged(packed)
    parts = [expert_quarter_many(received, gate_up, down)]
    for step in range(1, group_count):
        parts.append(shifted(expert_quarter_many(shifted(received, step), gate_up, down), -step))
    summed = move(exchanged(added(parts)), ("section",), lambda s: (s + 1,))
    return mix(share_table(meta, stream.shape[0], held_count), [summed])


def shards(stream, norm_gain, gate_probs, expert_ids, gate_up_weight, down_weight):
    paired = lax.axis_size("expert") == 2 and lax.axis_size("dp") == 4
    body = pair_shards if paired else many_shards
    return body(
        stream[0], norm_gain, gate_probs[0].T, expert_ids[0].T, gate_up_weight[0, 0], down_weight[0, 0]
    )[None]


def solution(mesh):
    in_specs = (
        P("section", ("dp", "expert"), None),
        P("section", None),
        P("section", ("dp", "expert"), None),
        P("section", ("dp", "expert"), None),
        P("section", "expert", None, None, "dp"),
        P("section", "expert", "dp", None),
    )
    out_specs = P("section", ("dp", "expert"), None)
    return jax.shard_map(shards, mesh=mesh, in_specs=in_specs, out_specs=out_specs, check_vma=False)
```

```python
import functools

import jax
import jax.numpy as jnp
from jax import lax
from jax.experimental import pallas as pl
from jax.experimental.pallas import tpu as pltpu
from jax.sharding import PartitionSpec as P

CAP = 12
GROUP = 2 * CAP
epsilon = 1e-06
f32 = jnp.float32
bf16 = jnp.bfloat16
LOAD_PIECES = 2
MIX_PIECES = 2
VMEM_LIMIT = 40 * 1024 * 1024
LIGHT = pl.CostEstimate(flops=1, bytes_accessed=1, transcendentals=0)


def row_tables(rows, lanes):
    row = lax.broadcasted_iota(jnp.int32, (rows, lanes), 0) % GROUP
    left = (row < 8) | ((row >= 16) & (row < 20))
    slot = jnp.where(row < 8, row, jnp.where(row < 20, row - 8, row - 12))
    return left, slot


def swap_halves(value):
    pieces = []
    for first in range(0, value.shape[0], GROUP):
        pieces.append(value[first + 8 : first + 16])
        pieces.append(value[first : first + 8])
        pieces.append(pltpu.roll(value[first + 16 : first + 24], 4, 0))
    return jnp.concatenate(pieces, axis=0)


def dot(left, right):
    return jnp.dot(left, right, preferred_element_type=f32)


def pack_kernel(base_ref, ids_hbm, probs_hbm, stream_hbm, gain_hbm, gate_up_hbm, down_hbm, meta_ref, *refs, held_count):
    packed_refs = refs[:-7]
    gate_up_ref, down_ref = refs[-7:-5]
    ids_ref, probs_ref, stream_ref, gain_ref, sems = refs[-5:]
    pairs = [(ids_hbm, ids_ref), (probs_hbm, probs_ref), (stream_hbm, stream_ref), (gain_hbm, gain_ref)]
    depth = gate_up_ref.shape[1] // LOAD_PIECES
    for matrix in range(2):
        for piece in range(LOAD_PIECES):
            place = (matrix, pl.ds(piece * depth, depth))
            pairs.append((gate_up_hbm.at[place], gate_up_ref.at[place]))
    depth = down_ref.shape[0] // LOAD_PIECES
    for piece in range(LOAD_PIECES):
        place = pl.ds(piece * depth, depth)
        pairs.append((down_hbm.at[place], down_ref.at[place]))
    copies = [
        pltpu.make_async_copy(source, target, sems.at[index]) for index, (source, target) in enumerate(pairs)
    ]
    for copy in copies:
        copy.start()
    copies[0].wait()
    copies[1].wait()
    ids = ids_ref[...]
    probs = probs_ref[...]
    weights = probs / jnp.sum(probs, axis=0, keepdims=True)
    tokens = ids.shape[1]
    half = stream_ref.shape[1] // 2
    chosen, coefficients = [], []
    for block in range(held_count):
        matches = ids == lax.rem(base_ref[0] + block, held_count)
        coefficients.append(jnp.sum(jnp.where(matches, weights, 0.0), axis=0, keepdims=True))
        chosen.append(jnp.sum(jnp.where(matches, 1.0, 0.0), axis=0, keepdims=True))
    padding = -held_count % 8
    stacked = jnp.concatenate(chosen + [jnp.zeros((padding, tokens), f32)] * (padding > 0), axis=0)
    earlier = lax.broadcasted_iota(jnp.int32, (tokens, tokens), 0) < lax.broadcasted_iota(
        jnp.int32, (tokens, tokens), 1
    )
    counted = dot(stacked.astype(bf16), jnp.where(earlier, 1.0, 0.0).astype(bf16))
    position = jnp.where(stacked > 0.5, counted, -1.0)
    rows = held_count * GROUP
    left, slot = row_tables(rows, tokens)
    spread = jnp.concatenate(
        [jnp.broadcast_to(position[e : e + 1], (GROUP, tokens)) for e in range(held_count)], axis=0
    )
    onehot = slot.astype(f32) == spread
    lines = []
    for block in range(held_count):
        rest = coefficients[block]
        for _ in range(3):
            piece = rest.astype(bf16).astype(f32)
            lines.append(piece)
            rest = rest - piece
        lines.append(position[block : block + 1])
    meta_ref[...] = jnp.concatenate(lines, axis=0).astype(bf16)
    copies[2].wait()
    packed = dot(jnp.where(onehot & left, 1.0, 0.0).astype(bf16), stream_ref[:, :half])
    packed += dot(jnp.where(onehot & ~left, 1.0, 0.0).astype(bf16), stream_ref[:, half:])
    squares = packed * packed
    total = jnp.sum(squares + swap_halves(squares), axis=1, keepdims=True)
    inverse_rms = lax.rsqrt(total / (2 * half) + epsilon)
    copies[3].wait()
    gain = gain_ref[...].astype(f32)
    left, _ = row_tables(rows, half)
    normed = packed * inverse_rms * jnp.where(left, gain[:, :half], gain[:, half:])
    per_ref = rows // len(packed_refs)
    for index, ref in enumerate(packed_refs):
        ref[...] = normed[index * per_ref : (index + 1) * per_ref].astype(bf16)
    for copy in copies[4:]:
        copy.wait()


def pack(stream, gain, probs, ids, gate_up, down, base, held_count, outputs):
    tokens, width = stream.shape
    rows = held_count * GROUP // outputs
    whole = pl.BlockSpec(memory_space=pltpu.VMEM)
    far = pl.BlockSpec(memory_space=pltpu.HBM)
    arrays = (ids, probs, stream, gain, gate_up, down)
    return pl.pallas_call(
        functools.partial(pack_kernel, held_count=held_count),
        out_shape=[jax.ShapeDtypeStruct((4 * held_count, tokens), bf16)]
        + [jax.ShapeDtypeStruct((rows, width // 2), bf16)] * outputs
        + [jax.ShapeDtypeStruct(gate_up.shape, bf16), jax.ShapeDtypeStruct(down.shape, bf16)],
        in_specs=[pl.BlockSpec(memory_space=pltpu.SMEM)] + [far] * len(arrays),
        out_specs=[whole] * (3 + outputs),
        scratch_shapes=[pltpu.VMEM(array.shape, array.dtype) for array in arrays[:4]]
        + [pltpu.SemaphoreType.DMA((4 + 3 * LOAD_PIECES,))],
        compiler_params=pltpu.CompilerParams(vmem_limit_bytes=VMEM_LIMIT),
    )(base, *[pltpu.with_memory_space_constraint(array, pltpu.HBM) for array in arrays])


def expert_rows(value, gate_ref, up_ref, down_ref):
    half = value.shape[1]
    value = value.astype(f32)
    swapped = swap_halves(value)
    left, _ = row_tables(*value.shape)
    first = jnp.where(left, value, swapped).astype(bf16)
    second = jnp.where(left, swapped, value).astype(bf16)
    gate = dot(first, gate_ref[:half]) + dot(second, gate_ref[half:])
    up = dot(first, up_ref[:half]) + dot(second, up_ref[half:])
    hidden = (gate / (1.0 + jnp.exp(-gate)) * up).astype(bf16)
    result = dot(hidden, down_ref[...])
    return jnp.where(left, result[:, :half], result[:, half:])


def expert_kernel(gate_up_ref, down_ref, *refs, count):
    value = jnp.concatenate([ref[...].astype(f32) for ref in refs[:count]], axis=0)
    result = expert_rows(value, gate_up_ref.at[0], gate_up_ref.at[1], down_ref)
    first = 0
    for ref in refs[count:]:
        ref[...] = result[first : first + ref.shape[0]].astype(bf16)
        first += ref.shape[0]


def expert_quarter(blocks, out_rows, gate_up, down):
    width = blocks[0].shape[1]
    whole = pl.BlockSpec(memory_space=pltpu.VMEM)
    return pl.pallas_call(
        functools.partial(expert_kernel, count=len(blocks)),
        out_shape=[jax.ShapeDtypeStruct((count, width), bf16) for count in out_rows],
        in_specs=[whole] * (2 + len(blocks)),
        out_specs=[whole] * len(out_rows),
        cost_estimate=LIGHT,
        compiler_params=pltpu.CompilerParams(vmem_limit_bytes=VMEM_LIMIT),
    )(gate_up, down, *blocks)


def many_kernel(gate_up_ref, down_ref, in_ref, out_ref):
    out_ref[...] = expert_rows(in_ref[...], gate_up_ref.at[0], gate_up_ref.at[1], down_ref).astype(bf16)


def expert_quarter_many(block, gate_up, down):
    rows, width = block.shape
    step = GROUP * 4 if rows % (GROUP * 4) == 0 else rows
    return pl.pallas_call(
        many_kernel,
        grid=(rows // step,),
        out_shape=jax.ShapeDtypeStruct((rows, width), bf16),
        in_specs=[
            pl.BlockSpec(gate_up.shape, lambda i: (0, 0, 0)),
            pl.BlockSpec(down.shape, lambda i: (0, 0)),
            pl.BlockSpec((step, width), lambda i: (i, 0)),
        ],
        out_specs=pl.BlockSpec((step, width), lambda i: (i, 0)),
        compiler_params=pltpu.CompilerParams(vmem_limit_bytes=VMEM_LIMIT),
    )(gate_up, down, block)


def mix_kernel(meta_ref, *refs, held_count):
    rows_refs, out_hbm, out_ref, sems = refs[:-3], refs[-3], refs[-2], refs[-1]
    tokens, width = out_ref.shape
    half = width // 2
    meta = meta_ref[:, :tokens].astype(f32)
    _, slot = row_tables(GROUP, tokens)
    values = jnp.concatenate([ref[...].astype(f32) for ref in rows_refs], axis=0)
    left, _ = row_tables(*values.shape)
    sides = [jnp.where(left, values, 0.0).astype(bf16), jnp.where(left, 0.0, values).astype(bf16)]
    lines = []
    for piece in range(3):
        for block in range(held_count):
            position = meta[4 * block + 3 : 4 * block + 4]
            share = meta[4 * block + piece : 4 * block + piece + 1]
            lines.append(jnp.where(slot.astype(f32) == position, share, 0.0))
    table = jnp.concatenate(lines, axis=0).T.astype(bf16)
    copies = []
    for step in range(2 * MIX_PIECES):
        side, piece = divmod(step, MIX_PIECES)
        length = half // MIX_PIECES
        columns = pl.ds(step * length, length)
        value = sides[side][:, piece * length : (piece + 1) * length]
        total = dot(table, jnp.concatenate([value] * 3, axis=0))
        out_ref[:, columns] = total.astype(bf16)
        copies.append(pltpu.make_async_copy(out_ref.at[:, columns], out_hbm.at[:, columns], sems.at[step]))
        copies[step].start()
    for copy in copies:
        copy.wait()


def mix(meta, blocks, tokens, held_count):
    width = blocks[0].shape[1]
    whole = pl.BlockSpec(memory_space=pltpu.VMEM)
    return pl.pallas_call(
        functools.partial(mix_kernel, held_count=held_count),
        out_shape=jax.ShapeDtypeStruct((tokens, 2 * width), bf16),
        in_specs=[whole] * (1 + len(blocks)),
        out_specs=pl.BlockSpec(memory_space=pltpu.HBM),
        scratch_shapes=[pltpu.VMEM((tokens, 2 * width), bf16), pltpu.SemaphoreType.DMA((2 * MIX_PIECES,))],
        compiler_params=pltpu.CompilerParams(vmem_limit_bytes=VMEM_LIMIT),
    )(meta, *blocks)


def move(value, axes, target):
    sizes = [lax.axis_size(axis) for axis in axes]
    pairs = []
    total = 1
    for size in sizes:
        total *= size
    for source in range(total):
        rest, place = source, []
        for size in reversed(sizes):
            place.insert(0, rest % size)
            rest //= size
        index = 0
        for size, coordinate in zip(sizes, target(*place)):
            index = index * size + coordinate % size
        pairs.append((source, index))
    return lax.ppermute(value, axes if len(axes) > 1 else axes[0], pairs)


def across(value, step):
    return move(value, ("dp",), lambda q: (q ^ step,))


def added(values):
    total = values[0].astype(f32)
    for value in values[1:]:
        total = total + value.astype(f32)
    return total.astype(bf16)


def pair_shards(stream, gain, probs, ids, gate_up, down):
    base = lax.axis_index("expert").astype(jnp.int32).reshape(1)
    meta, own, other, gate_up, down = pack(stream, gain, probs, ids, gate_up, down, base, 2, 2)
    other = move(other, ("expert",), lambda e: (e ^ 1,))
    blocks = {0: [own, other]}
    for step in (3, 2, 1):
        blocks[step] = [across(own, step), across(other, step)]
    rows = [2 * GROUP] * 2
    part1, part3 = expert_quarter(blocks[1] + blocks[3], rows, gate_up, down)
    part0, part2 = expert_quarter(blocks[0] + blocks[2], rows, gate_up, down)
    summed = added([part0, across(part1, 1), across(part3, 3)])
    direct = move(part2[:GROUP], ("section", "dp"), lambda s, q: (s + 1, q ^ 2))
    direct_crossed = move(part2[GROUP:], ("section", "dp", "expert"), lambda s, q, e: (s + 1, q ^ 2, e ^ 1))
    wide = jnp.pad(meta, ((0, 0), (0, summed.shape[1] - meta.shape[1])))
    tagged = jnp.concatenate([summed[:GROUP], wide], axis=0)
    tagged = move(tagged, ("section",), lambda s: (s + 1,))
    crossed = move(summed[GROUP:], ("section", "expert"), lambda s, e: (s + 1, e ^ 1))
    return mix(tagged[GROUP:], [added([tagged[:GROUP], direct]), added([crossed, direct_crossed])], stream.shape[0], 2)


def many_shards(stream, gain, probs, ids, gate_up, down):
    held_count = lax.axis_size("expert")
    group_count = lax.axis_size("dp")
    base = jnp.zeros((1,), jnp.int32)
    meta, packed, gate_up, down = pack(stream, gain, probs, ids, gate_up, down, base, held_count, 1)
    meta = move(meta, ("section",), lambda s: (s + 1,))
    shape = packed.shape
    split = (held_count, GROUP, shape[1])

    def exchanged(value):
        return lax.all_to_all(value.reshape(split), "expert", split_axis=0, concat_axis=0, tiled=True).reshape(shape)

    def shifted(value, step):
        return move(value, ("dp",), lambda q: (q + step,))

    received = exchanged(packed)
    parts = [expert_quarter_many(received, gate_up, down)]
    for step in range(1, group_count):
        parts.append(shifted(expert_quarter_many(shifted(received, step), gate_up, down), -step))
    summed = move(exchanged(added(parts)), ("section",), lambda s: (s + 1,))
    return mix(meta, [summed], stream.shape[0], held_count)


def shards(stream, norm_gain, gate_probs, expert_ids, gate_up_weight, down_weight):
    paired = lax.axis_size("expert") == 2 and lax.axis_size("dp") == 4
    body = pair_shards if paired else many_shards
    return body(
        stream[0], norm_gain, gate_probs[0].T, expert_ids[0].T, gate_up_weight[0, 0], down_weight[0, 0]
    )[None]


def solution(mesh):
    in_specs = (
        P("section", ("dp", "expert"), None),
        P("section", None),
        P("section", ("dp", "expert"), None),
        P("section", ("dp", "expert"), None),
        P("section", "expert", None, None, "dp"),
        P("section", "expert", "dp", None),
    )
    out_specs = P("section", ("dp", "expert"), None)
    return jax.shard_map(shards, mesh=mesh, in_specs=in_specs, out_specs=out_specs, check_vma=False)
```

```python
import functools

import jax
import jax.numpy as jnp
from jax import lax
from jax.experimental import pallas as pl
from jax.experimental.pallas import tpu as pltpu
from jax.sharding import PartitionSpec as P

CAP = 12
GROUP = 2 * CAP
epsilon = 1e-06
f32 = jnp.float32
bf16 = jnp.bfloat16
LOAD_PIECES = 2
MIX_PIECES = 2
VMEM_LIMIT = 40 * 1024 * 1024
LIGHT = pl.CostEstimate(flops=1, bytes_accessed=1, transcendentals=0)


def row_tables(rows, lanes):
    row = lax.broadcasted_iota(jnp.int32, (rows, lanes), 0) % GROUP
    left = (row < 8) | ((row >= 16) & (row < 20))
    slot = jnp.where(row < 8, row, jnp.where(row < 20, row - 8, row - 12))
    return left, slot


def swap_halves(value):
    pieces = []
    for first in range(0, value.shape[0], GROUP):
        pieces.append(value[first + 8 : first + 16])
        pieces.append(value[first : first + 8])
        pieces.append(pltpu.roll(value[first + 16 : first + 24], 4, 0))
    return jnp.concatenate(pieces, axis=0)


def dot(left, right):
    return jnp.dot(left, right, preferred_element_type=f32)


def pack_kernel(base_ref, ids_hbm, probs_hbm, stream_hbm, gain_hbm, gate_up_hbm, down_hbm, meta_ref, *refs, held_count):
    packed_refs = refs[:-7]
    gate_up_ref, down_ref = refs[-7:-5]
    ids_ref, probs_ref, stream_ref, gain_ref, sems = refs[-5:]
    pairs = [(ids_hbm, ids_ref), (probs_hbm, probs_ref), (stream_hbm, stream_ref), (gain_hbm, gain_ref)]
    depth = gate_up_ref.shape[1] // LOAD_PIECES
    for matrix in range(2):
        for piece in range(LOAD_PIECES):
            place = (matrix, pl.ds(piece * depth, depth))
            pairs.append((gate_up_hbm.at[place], gate_up_ref.at[place]))
    depth = down_ref.shape[0] // LOAD_PIECES
    for piece in range(LOAD_PIECES):
        place = pl.ds(piece * depth, depth)
        pairs.append((down_hbm.at[place], down_ref.at[place]))
    copies = [
        pltpu.make_async_copy(source, target, sems.at[index]) for index, (source, target) in enumerate(pairs)
    ]
    for copy in copies:
        copy.start()
    copies[0].wait()
    copies[1].wait()
    ids = ids_ref[...]
    probs = probs_ref[...]
    weights = probs / jnp.sum(probs, axis=0, keepdims=True)
    tokens = ids.shape[1]
    half = stream_ref.shape[1] // 2
    chosen, coefficients = [], []
    for block in range(held_count):
        matches = ids == lax.rem(base_ref[0] + block, held_count)
        coefficients.append(jnp.sum(jnp.where(matches, weights, 0.0), axis=0, keepdims=True))
        chosen.append(jnp.sum(jnp.where(matches, 1.0, 0.0), axis=0, keepdims=True))
    padding = -held_count % 8
    stacked = jnp.concatenate(chosen + [jnp.zeros((padding, tokens), f32)] * (padding > 0), axis=0)
    earlier = lax.broadcasted_iota(jnp.int32, (tokens, tokens), 0) < lax.broadcasted_iota(
        jnp.int32, (tokens, tokens), 1
    )
    counted = dot(stacked.astype(bf16), jnp.where(earlier, 1.0, 0.0).astype(bf16))
    position = jnp.where(stacked > 0.5, counted, -1.0)
    rows = held_count * GROUP
    left, slot = row_tables(rows, tokens)
    spread = jnp.concatenate(
        [jnp.broadcast_to(position[e : e + 1], (GROUP, tokens)) for e in range(held_count)], axis=0
    )
    onehot = slot.astype(f32) == spread
    lines = []
    for block in range(held_count):
        rest = coefficients[block]
        for _ in range(3):
            piece = rest.astype(bf16).astype(f32)
            lines.append(piece)
            rest = rest - piece
        lines.append(position[block : block + 1])
    meta_ref[...] = jnp.concatenate(lines, axis=0).astype(bf16)
    copies[2].wait()
    packed = dot(jnp.where(onehot & left, 1.0, 0.0).astype(bf16), stream_ref[:, :half])
    packed += dot(jnp.where(onehot & ~left, 1.0, 0.0).astype(bf16), stream_ref[:, half:])
    squares = packed * packed
    total = jnp.sum(squares + swap_halves(squares), axis=1, keepdims=True)
    inverse_rms = lax.rsqrt(total / (2 * half) + epsilon)
    copies[3].wait()
    gain = gain_ref[...].astype(f32)
    left, _ = row_tables(rows, half)
    normed = packed * inverse_rms * jnp.where(left, gain[:, :half], gain[:, half:])
    per_ref = rows // len(packed_refs)
    for index, ref in enumerate(packed_refs):
        ref[...] = normed[index * per_ref : (index + 1) * per_ref].astype(bf16)
    for copy in copies[4:]:
        copy.wait()


def pack(stream, gain, probs, ids, gate_up, down, base, held_count, outputs):
    tokens, width = stream.shape
    rows = held_count * GROUP // outputs
    whole = pl.BlockSpec(memory_space=pltpu.VMEM)
    far = pl.BlockSpec(memory_space=pltpu.HBM)
    arrays = (ids, probs, stream, gain, gate_up, down)
    return pl.pallas_call(
        functools.partial(pack_kernel, held_count=held_count),
        out_shape=[jax.ShapeDtypeStruct((4 * held_count, tokens), bf16)]
        + [jax.ShapeDtypeStruct((rows, width // 2), bf16)] * outputs
        + [jax.ShapeDtypeStruct(gate_up.shape, bf16), jax.ShapeDtypeStruct(down.shape, bf16)],
        in_specs=[pl.BlockSpec(memory_space=pltpu.SMEM)] + [far] * len(arrays),
        out_specs=[whole] * (3 + outputs),
        scratch_shapes=[pltpu.VMEM(array.shape, array.dtype) for array in arrays[:4]]
        + [pltpu.SemaphoreType.DMA((4 + 3 * LOAD_PIECES,))],
        compiler_params=pltpu.CompilerParams(vmem_limit_bytes=VMEM_LIMIT),
    )(base, *[pltpu.with_memory_space_constraint(array, pltpu.HBM) for array in arrays])


def expert_rows(value, gate_ref, up_ref, down_ref):
    half = value.shape[1]
    value = value.astype(f32)
    swapped = swap_halves(value)
    left, _ = row_tables(*value.shape)
    first = jnp.where(left, value, swapped).astype(bf16)
    second = jnp.where(left, swapped, value).astype(bf16)
    gate = dot(first, gate_ref[:half]) + dot(second, gate_ref[half:])
    up = dot(first, up_ref[:half]) + dot(second, up_ref[half:])
    hidden = (gate / (1.0 + jnp.exp(-gate)) * up).astype(bf16)
    result = dot(hidden, down_ref[...])
    return jnp.where(left, result[:, :half], result[:, half:])


def expert_kernel(gate_up_ref, down_ref, *refs, count):
    value = jnp.concatenate([ref[...].astype(f32) for ref in refs[:count]], axis=0)
    result = expert_rows(value, gate_up_ref.at[0], gate_up_ref.at[1], down_ref)
    first = 0
    for ref in refs[count:]:
        ref[...] = result[first : first + ref.shape[0]].astype(bf16)
        first += ref.shape[0]


def expert_quarter(blocks, out_rows, gate_up, down):
    width = blocks[0].shape[1]
    whole = pl.BlockSpec(memory_space=pltpu.VMEM)
    return pl.pallas_call(
        functools.partial(expert_kernel, count=len(blocks)),
        out_shape=[jax.ShapeDtypeStruct((count, width), bf16) for count in out_rows],
        in_specs=[whole] * (2 + len(blocks)),
        out_specs=[whole] * len(out_rows),
        cost_estimate=LIGHT,
        compiler_params=pltpu.CompilerParams(vmem_limit_bytes=VMEM_LIMIT),
    )(gate_up, down, *blocks)


def many_kernel(gate_up_ref, down_ref, in_ref, out_ref):
    out_ref[...] = expert_rows(in_ref[...], gate_up_ref.at[0], gate_up_ref.at[1], down_ref).astype(bf16)


def expert_quarter_many(block, gate_up, down):
    rows, width = block.shape
    step = GROUP * 4 if rows % (GROUP * 4) == 0 else rows
    return pl.pallas_call(
        many_kernel,
        grid=(rows // step,),
        out_shape=jax.ShapeDtypeStruct((rows, width), bf16),
        in_specs=[
            pl.BlockSpec(gate_up.shape, lambda i: (0, 0, 0)),
            pl.BlockSpec(down.shape, lambda i: (0, 0)),
            pl.BlockSpec((step, width), lambda i: (i, 0)),
        ],
        out_specs=pl.BlockSpec((step, width), lambda i: (i, 0)),
        compiler_params=pltpu.CompilerParams(vmem_limit_bytes=VMEM_LIMIT),
    )(gate_up, down, block)


def mix_kernel(meta_ref, *refs, held_count):
    rows_refs, out_hbm, out_ref, sems = refs[:-3], refs[-3], refs[-2], refs[-1]
    tokens, width = out_ref.shape
    half = width // 2
    meta = meta_ref[:, :tokens].astype(f32)
    _, slot = row_tables(GROUP, tokens)
    values = jnp.concatenate([ref[...].astype(f32) for ref in rows_refs], axis=0)
    left, _ = row_tables(*values.shape)
    sides = [jnp.where(left, values, 0.0).astype(bf16), jnp.where(left, 0.0, values).astype(bf16)]
    lines = []
    for piece in range(3):
        for block in range(held_count):
            position = meta[4 * block + 3 : 4 * block + 4]
            share = meta[4 * block + piece : 4 * block + piece + 1]
            lines.append(jnp.where(slot.astype(f32) == position, share, 0.0))
    table = jnp.concatenate(lines, axis=0).T.astype(bf16)
    copies = []
    for step in range(2 * MIX_PIECES):
        side, piece = divmod(step, MIX_PIECES)
        length = half // MIX_PIECES
        columns = pl.ds(step * length, length)
        value = sides[side][:, piece * length : (piece + 1) * length]
        total = dot(table, jnp.concatenate([value] * 3, axis=0))
        out_ref[:, columns] = total.astype(bf16)
        copies.append(pltpu.make_async_copy(out_ref.at[:, columns], out_hbm.at[:, columns], sems.at[step]))
        copies[step].start()
    for copy in copies:
        copy.wait()


def mix(meta, blocks, tokens, held_count):
    width = blocks[0].shape[1]
    whole = pl.BlockSpec(memory_space=pltpu.VMEM)
    return pl.pallas_call(
        functools.partial(mix_kernel, held_count=held_count),
        out_shape=jax.ShapeDtypeStruct((tokens, 2 * width), bf16),
        in_specs=[whole] * (1 + len(blocks)),
        out_specs=pl.BlockSpec(memory_space=pltpu.HBM),
        scratch_shapes=[pltpu.VMEM((tokens, 2 * width), bf16), pltpu.SemaphoreType.DMA((2 * MIX_PIECES,))],
        compiler_params=pltpu.CompilerParams(vmem_limit_bytes=VMEM_LIMIT),
    )(meta, *blocks)


def move(value, axes, target):
    sizes = [lax.axis_size(axis) for axis in axes]
    pairs = []
    total = 1
    for size in sizes:
        total *= size
    for source in range(total):
        rest, place = source, []
        for size in reversed(sizes):
            place.insert(0, rest % size)
            rest //= size
        index = 0
        for size, coordinate in zip(sizes, target(*place)):
            index = index * size + coordinate % size
        pairs.append((source, index))
    return lax.ppermute(value, axes if len(axes) > 1 else axes[0], pairs)


def across(value, step):
    return move(value, ("dp",), lambda q: (q ^ step,))


def swapped_across(value, step):
    return move(value, ("dp", "expert"), lambda q, e: (q ^ step, e ^ 1))


def added(values):
    total = values[0].astype(f32)
    for value in values[1:]:
        total = total + value.astype(f32)
    return total.astype(bf16)


def pair_shards(stream, gain, probs, ids, gate_up, down):
    base = lax.axis_index("expert").astype(jnp.int32).reshape(1)
    meta, own, other, gate_up, down = pack(stream, gain, probs, ids, gate_up, down, base, 2, 2)
    mine = other
    other = move(other, ("expert",), lambda e: (e ^ 1,))
    blocks = {0: [own, other]}
    for step in (3, 2, 1):
        blocks[step] = [across(own, step), swapped_across(mine, step)]
    rows = [2 * GROUP] * 2
    part0, part2 = expert_quarter(blocks[0] + blocks[2], rows, gate_up, down)
    part1, part3 = expert_quarter(blocks[1] + blocks[3], rows, gate_up, down)
    summed = added([part0, across(part1, 1), across(part3, 3)])
    direct = move(part2[:GROUP], ("section", "dp"), lambda s, q: (s + 1, q ^ 2))
    direct_crossed = move(part2[GROUP:], ("section", "dp", "expert"), lambda s, q, e: (s + 1, q ^ 2, e ^ 1))
    wide = jnp.pad(meta, ((0, 0), (0, summed.shape[1] - meta.shape[1])))
    tagged = jnp.concatenate([summed[:GROUP], wide], axis=0)
    tagged = move(tagged, ("section",), lambda s: (s + 1,))
    crossed = move(summed[GROUP:], ("section", "expert"), lambda s, e: (s + 1, e ^ 1))
    return mix(tagged[GROUP:], [added([tagged[:GROUP], direct]), added([crossed, direct_crossed])], stream.shape[0], 2)


def many_shards(stream, gain, probs, ids, gate_up, down):
    held_count = lax.axis_size("expert")
    group_count = lax.axis_size("dp")
    base = jnp.zeros((1,), jnp.int32)
    meta, packed, gate_up, down = pack(stream, gain, probs, ids, gate_up, down, base, held_count, 1)
    meta = move(meta, ("section",), lambda s: (s + 1,))
    shape = packed.shape
    split = (held_count, GROUP, shape[1])

    def exchanged(value):
        return lax.all_to_all(value.reshape(split), "expert", split_axis=0, concat_axis=0, tiled=True).reshape(shape)

    def shifted(value, step):
        return move(value, ("dp",), lambda q: (q + step,))

    received = exchanged(packed)
    parts = [expert_quarter_many(received, gate_up, down)]
    for step in range(1, group_count):
        parts.append(shifted(expert_quarter_many(shifted(received, step), gate_up, down), -step))
    summed = move(exchanged(added(parts)), ("section",), lambda s: (s + 1,))
    return mix(meta, [summed], stream.shape[0], held_count)


def shards(stream, norm_gain, gate_probs, expert_ids, gate_up_weight, down_weight):
    paired = lax.axis_size("expert") == 2 and lax.axis_size("dp") == 4
    body = pair_shards if paired else many_shards
    return body(
        stream[0], norm_gain, gate_probs[0].T, expert_ids[0].T, gate_up_weight[0, 0], down_weight[0, 0]
    )[None]


def solution(mesh):
    in_specs = (
        P("section", ("dp", "expert"), None),
        P("section", None),
        P("section", ("dp", "expert"), None),
        P("section", ("dp", "expert"), None),
        P("section", "expert", None, None, "dp"),
        P("section", "expert", "dp", None),
    )
    out_specs = P("section", ("dp", "expert"), None)
    return jax.shard_map(shards, mesh=mesh, in_specs=in_specs, out_specs=out_specs, check_vma=False)
```
